128 devices in a mesh: dp: 8 (over y, x_lo), feat: 16 (over z, x_hi, core).
Axes of the slice: x: 4 (x_hi: 2, x_lo: 2; x = x_hi * 2 + x_lo), y: 4, z: 4, core: 2. Of those that a mesh axis runs over, the one named last changes fastest.
Arguments:
- fisher: bfloat16 [4096, 32768], P('dp', 'feat'), may hold values from -0.03125 to 0.03125
- sample_ids: int32 [4096], P('dp'), may hold values from 0 to 511
- labels: int32 [4096, 604], P('dp'), may hold values 0 or 1
- weights: bfloat16 [32768, 604], P('feat'), may hold values from -26 to 26
Outputs:
- newton_step: float32 [16, 2048, 604], P('feat', 'dp')
- residual: float32 [16, 2048, 604], P('feat', 'dp')
The draws below stay inside these ranges and needn't reach their ends.
Inputs may be any that keep to these rules, and one draw needn't show every extreme that they name: `sample_ids`: each entry names a row of its own aligned block of 512 rows of fisher, counted from the block's start; rows may repeat.
All inputs are finite; a program needn't handle non-finite values. No bound on the sum of `labels` on one device may be relied on, other than what follows from the above.
Results may differ from the reference program's by a relative error of at most 0.0005.
Values sent between devices are 32-bit elements; how exact they have to be, the bound alone decides.
No kernel may reach another device: no remote copies, remote signals or barrier semaphores. Data moves between devices by JAX's collectives and lax.ppermute only.
A program may use at most 64 MiB of HBM per device.

```python
import jax
import jax.numpy as jnp
from jax import lax

F = 32768
L = 604
ROWS_DEV = 512
ITERS = 3
ROWS = 4096
N_DP = 8
N_FEAT = 16


def draw_weights(key, part):
    key = jax.random.fold_in(key, 5)
    key_base, key_cols, key_rough = jax.random.split(key, 3)
    columns = jnp.exp(jax.random.uniform(key_cols, (1, L), jnp.float32, jnp.log(0.3), jnp.log(3.0)))
    ramp = 0.5 + jnp.arange(F, dtype=jnp.float32)[:, None] / F
    rough = jnp.exp(jax.random.uniform(key_rough, (F, 1), jnp.float32, -0.35, 0.35))
    base = jnp.clip(jax.random.normal(key_base, (F, L), jnp.float32), -4.0, 4.0)
    return (base * columns * ramp * rough).astype(jnp.bfloat16)


def with_ends(entries, own_key, smallest, largest):
    longest = entries.shape.index(max(entries.shape))
    spots = []
    for shift in (0, 1):
        where = [jax.random.randint(jax.random.fold_in(own_key, axis), (), 0, length) for axis, length in enumerate(entries.shape)]
        where[longest] = (where[longest] + shift) % entries.shape[longest]
        spots.append(tuple(where))
    return entries.at[spots[0]].set(smallest).at[spots[1]].set(largest)


def level_of(rng, dims, pieces, smallest, largest):
    loudness = 1.0
    for dim, parts in pieces:
        heights = jax.random.uniform(jax.random.fold_in(jax.random.fold_in(rng, 6), dim), (parts,), jnp.float32, smallest / len(pieces), largest / len(pieces))
        loudness = loudness * jnp.repeat(jnp.exp(heights), dims[dim] // parts).reshape((-1,) + (1,) * (len(dims) - 1 - dim))
    return loudness


def noise(key, dims, width, limit, cuts=(), held_as=jnp.bfloat16):
    drawn = width * jax.random.normal(key, dims, jnp.float32)
    if cuts:
        drawn = drawn * level_of(key, dims, cuts, -0.22, 0.18)
    return jnp.clip(drawn, -limit, limit).astype(held_as)


def setup_inputs(seed: int = 0) -> dict:
    key_list = jax.random.split(jax.random.key(seed), 5)
    return {
        "fisher": noise(key_list[0], (ROWS, F), F ** -0.5, 0.03125, ((0, 8), (1, 16))),
        "sample_ids": with_ends(jax.random.randint(key_list[1], (ROWS,), 0, ROWS_DEV), jax.random.fold_in(key_list[1], 1), 0, ROWS_DEV - 1).astype(jnp.int32),
        "labels": with_ends((jax.random.randint(key_list[2], (ROWS, L), 0, 4) < 1).astype(jnp.int32), jax.random.fold_in(key_list[2], 1), 0, 1),
        "weights": draw_weights(jax.random.fold_in(key_list[4], 71), 0),
    }


PENALTY = 8.0


def reference(fisher, sample_ids, labels, weights):
    offsets = jnp.repeat(jnp.arange(N_DP, dtype=jnp.int32) * ROWS_DEV, ROWS_DEV)
    global_ids = (sample_ids.astype(jnp.int32) + offsets).astype(jnp.int32)
    picked = fisher[global_ids].astype(jnp.float32)
    label_sign = 2.0 * labels.astype(jnp.float32) - 1.0
    highest = lax.Precision.HIGHEST

    def forward(matrix):
        return jnp.dot(picked, matrix, precision=highest, preferred_element_type=jnp.float32)

    def backward(values):
        return lax.dot_general(picked, values, (((0,), (0,)), ((), ())), precision=highest,
                               preferred_element_type=jnp.float32)

    start_weights = weights.astype(jnp.float32)
    margins = forward(start_weights)
    fit = jax.nn.sigmoid(label_sign * margins)
    loss_weight = PENALTY * (fit - 1.0) * label_sign
    curv_scale = PENALTY * fit * (1.0 - fit)
    gradient = start_weights + backward(loss_weight)

    def hessian(vector):
        product = forward(vector)
        return vector + backward(curv_scale * product)

    newton_step = jnp.zeros_like(gradient)
    residual = -gradient
    direction = residual
    norm_now = jnp.sum(residual * residual, axis=0)
    for iteration in range(ITERS):
        image = hessian(direction)
        alpha = norm_now / jnp.sum(direction * image, axis=0)
        newton_step = newton_step + alpha * direction
        residual = residual - alpha * image
        norm_next = jnp.sum(residual * residual, axis=0)
        direction = residual + (norm_next / norm_now) * direction
        norm_now = norm_next
    shape_out = (N_FEAT, F // N_FEAT, L)
    return newton_step.reshape(shape_out), residual.reshape(shape_out)
```

```python
import jax
import jax.numpy as jnp
from jax import lax
from jax.sharding import PartitionSpec as P

ITERS = 3
PENALTY = 8.0
NY, NX, NZ, NH, NC = 4, 2, 4, 2, 2
CHUNKS = 4
PIECE = 32


def dp_move(value, dy, dx=0):
    pairs = [(y * NX + x, ((y + dy) % NY) * NX + (x + dx) % NX) for y in range(NY) for x in range(NX)]
    return lax.ppermute(value, "dp", pairs)


def feat_move(value, dz, dh, dc):
    pairs = [
        ((z * NH + h) * NC + c, (((z + dz) % NZ) * NH + (h + dh) % NH) * NC + (c + dc) % NC)
        for z in range(NZ) for h in range(NH) for c in range(NC)
    ]
    return lax.ppermute(value, "feat", pairs)


def core_swap(value):
    return feat_move(value, 0, 0, 1)


OFFSETS = [(dz, dh) for dz in range(NZ) for dh in range(NH)]


def halves(value):
    high = lax.reduce_precision(value, 8, 7)
    return jnp.concatenate([high.astype(jnp.bfloat16), (value - high).astype(jnp.bfloat16)], axis=0)


def product(value, matrix, dim):
    both = lax.dot_general(halves(value), matrix, (((1,), (dim,)), ((), ())), preferred_element_type=jnp.float32)
    count = value.shape[0]
    return both[:count] + both[count:]


def to_tile(vectors):
    rows = [jnp.pad(v, (0, 256 - v.shape[0])).reshape(2, 128) for v in vectors]
    tile = jnp.concatenate(rows, axis=0)
    return jnp.pad(tile, ((0, 8 - tile.shape[0]), (0, 0)))


def from_tile(tile, place, count):
    return tile[2 * place:2 * place + 2].reshape(256)[:count]


def shards(fisher, sample_ids, labels, weights):
    dp = lax.axis_index("dp")
    feat = lax.axis_index("feat")
    y, x = dp // NX, dp % NX
    z, h, c = feat // (NH * NC), (feat // NC) % NH, feat % NC
    rows, width = fisher.shape
    classes = labels.shape[1]
    group = classes // NY
    held = group + (-group) % 8
    chunk = width // CHUNKS

    ids = sample_ids.reshape(NC, NZ, NH, PIECE)
    ids = jnp.where(c == 1, ids[::-1], ids)
    ids = lax.dynamic_slice_in_dim(jnp.concatenate([ids, ids], axis=1), z, NZ, 1)
    ids = jnp.where(h == 1, ids[:, :, ::-1], ids)
    picked = jnp.take(fisher, ids.reshape(rows), axis=0, mode="clip")

    blocks = []
    half = rows // 2
    for k in range(CHUNKS):
        with jax.named_scope("rows_along_y"):
            own = picked[:, k * chunk:(k + 1) * chunk]
            wide = 2.0 * own.astype(jnp.float32)
            before = dp_move(wide, 1)
            after = dp_move(wide, -1)
            far_a = dp_move(before[:half], 1)
            far_b = dp_move(after[half:], -1)
            far = jnp.concatenate([far_a, far_b], axis=0)
            slots = [own] + [(0.5 * v).astype(jnp.bfloat16) for v in (before, far, after)]
            pieces = [v.reshape(NC * NZ * NH, 1, PIECE, chunk) for v in slots]
            blocks.append(jnp.concatenate(pieces, axis=1).reshape(NY * rows, chunk))

    with jax.named_scope("margins"):
        partial = jnp.dot(picked, weights, preferred_element_type=jnp.float32)
        partial = partial[:half] + core_swap(partial[half:])
        summed = partial[:PIECE]
        for place, (dz, dh) in enumerate(OFFSETS):
            if place:
                summed = summed + feat_move(partial[place * PIECE:(place + 1) * PIECE], dz, dh, 0)
        own_labels = lax.dynamic_slice_in_dim(labels, ((c * NZ + z) * NH + h) * PIECE, PIECE, 0)
        label_sign = 2.0 * own_labels.astype(jnp.float32) - 1.0
        fit = jax.nn.sigmoid(label_sign * summed)
        loss_weight = PENALTY * (fit - 1.0) * label_sign
        curv = PENALTY * fit * (1.0 - fit)
        both = jnp.stack([loss_weight, curv]).reshape(2, PIECE, NY, group).transpose(2, 0, 3, 1)
        both = jnp.pad(both, ((0, 0), (0, 0), (0, held - group), (0, 0)))
        slots = []
        for k in range(NY):
            part = lax.dynamic_index_in_dim(both, (y + k) % NY, 0, keepdims=False)
            slots.append(part if k == 0 else dp_move(part, k))
        both = jnp.concatenate(slots, axis=2)
        loss_share, curv_share = both[0], both[1]

    def spread(share, tile):
        got = share if tile is None else jnp.concatenate([share, tile], axis=0)
        parts = [got] + [feat_move(got, -dz, -dh, 0) for dz, dh in OFFSETS[1:]]
        near = jnp.concatenate([v[:held] for v in parts], axis=1)
        whole = jnp.concatenate([near, core_swap(near)], axis=1)
        if tile is None:
            return whole, None
        total = parts[0][held:]
        for v in parts[1:]:
            total = total + v[held:]
        return whole, total + core_swap(total)

    def reduce(partial, tile):
        mid = partial.shape[1] // 2
        near = partial[:, :mid] + core_swap(partial[:, mid:])
        tile = tile + core_swap(tile)
        total = None
        for place, (dz, dh) in enumerate(OFFSETS):
            sent = jnp.concatenate([near[:, place * 128:(place + 1) * 128], tile], axis=0)
            got = sent if place == 0 else feat_move(sent, dz, dh, 0)
            total = got if total is None else total + got
        return total[:held], total[held:]

    with jax.named_scope("loss_spread"):
        loss_all, _ = spread(loss_share, None)

    own_weights = lax.dynamic_slice_in_dim(weights, y * group, group, 1).astype(jnp.float32).T
    own_weights = jnp.pad(own_weights, ((0, held - group), (0, 0)))

    residual = []
    partial, norm = 0.0, 0.0
    for k in range(CHUNKS):
        with jax.named_scope("gradient"):
            back = product(loss_all, blocks[k], 0)
            back = back + dp_move(back, 0, 1)
            value = -(own_weights[:, k * chunk:(k + 1) * chunk] + back)
            residual.append(value)
            norm = norm + jnp.sum(value * value, axis=1)
            partial = partial + product(value, blocks[k], 1)

    step = [0.0] * CHUNKS
    direction = swing = norm_now = None
    for iteration in range(ITERS):
        with jax.named_scope("sum_over_features"):
            mapped, tile = reduce(partial, to_tile([norm]))
            norm_next = from_tile(tile, 0, held)
        if iteration == 0:
            direction, swing = list(residual), mapped
        else:
            beta = (norm_next / norm_now)[:, None]
            direction = [r + beta * d for r, d in zip(residual, direction)]
            swing = mapped + beta * swing
        norm_now = norm_next
        with jax.named_scope("spread_scaled"):
            scaled = curv_share * swing
            curved = jnp.sum(scaled * swing, axis=1)
            plain = sum(jnp.sum(d * d, axis=1) for d in direction)
            scaled_all, tile = spread(scaled, to_tile([curved, plain]))
            curved = from_tile(tile, 0, held)
            curved = curved + dp_move(curved, 0, 1)
            alpha = (norm_now / (from_tile(tile, 1, held) + curved))[:, None]
        step = [n + alpha * d for n, d in zip(step, direction)]
        last = iteration == ITERS - 1
        partial, norm = 0.0, 0.0
        for k in range(CHUNKS):
            with jax.named_scope("image"):
                back = product(scaled_all, blocks[k], 0)
                if last:
                    share = chunk // NX
                    sent = lax.dynamic_slice_in_dim(back, (1 - x) * share, share, 1)
                    kept = lax.dynamic_slice_in_dim(back, x * share, share, 1)
                    image = lax.dynamic_slice_in_dim(direction[k], x * share, share, 1) + (kept + dp_move(sent, 0, 1))
                    residual[k] = lax.dynamic_slice_in_dim(residual[k], x * share, share, 1) - alpha * image
                    step[k] = lax.dynamic_slice_in_dim(step[k], x * share, share, 1)
                else:
                    image = direction[k] + (back + dp_move(back, 0, 1))
                    residual[k] = residual[k] - alpha * image
                    norm = norm + jnp.sum(residual[k] * residual[k], axis=1)
                    partial = partial + product(residual[k], blocks[k], 1)

    def place_out(parts):
        stacked = jnp.stack(parts)
        slots = []
        for k in range(NY):
            part = lax.dynamic_index_in_dim(stacked, (y + k) % NY, 0, keepdims=False)
            slots.append(part if k == 0 else dp_move(part, k))
        slots = jnp.stack(slots)
        ordered = [lax.dynamic_index_in_dim(slots, (y - g) % NY, 0, keepdims=False)[:group] for g in range(NY)]
        return jnp.concatenate(ordered, axis=0).T[None]

    with jax.named_scope("outputs"):
        return place_out(step), place_out(residual)


def solution(mesh):
    return jax.shard_map(
        shards,
        mesh=mesh,
        in_specs=(P("dp", "feat"), P("dp"), P("dp", None), P("feat", None)),
        out_specs=(P("feat", "dp", None), P("feat", "dp", None)),
        check_vma=False,
    )
```

```python
import jax
import jax.numpy as jnp
from jax import lax
from jax.sharding import Mesh, PartitionSpec as P

ITERS = 3
PENALTY = 8.0
SIZES = (4, 2, 4, 2, 2)
AXES = ("y", "l", "z", "h", "c")
NY, NL, NZ, NH, NC = SIZES
GROUP = ("l", "z", "h")
TEAM = NL * NZ * NH
PIECE = 32
PARTS = 2


def turn(value, axis, by):
    count = SIZES[AXES.index(axis)]
    return lax.ppermute(value, axis, [(i, (i + by) % count) for i in range(count)])


def halves(value):
    high = lax.reduce_precision(value, 8, 7)
    return jnp.concatenate([high.astype(jnp.bfloat16), (value - high).astype(jnp.bfloat16)], axis=0)


def product(both, matrix, dim):
    out = lax.dot_general(both, matrix, (((1,), (dim,)), ((), ())), preferred_element_type=jnp.float32)
    count = both.shape[0] // 2
    return out[:count] + out[count:]


def to_tile(vectors):
    rows = [jnp.pad(v, (0, 256 - v.shape[0])).reshape(2, 128) for v in vectors]
    tile = jnp.concatenate(rows, axis=0)
    return jnp.pad(tile, ((0, 8 - tile.shape[0]), (0, 0)))


def from_tile(tile, place, count):
    return tile[2 * place:2 * place + 2].reshape(256)[:count]


def shards(fisher, sample_ids, labels, weights):
    y, l, z, h, c = [lax.axis_index(a) for a in AXES]
    rows, width = fisher.shape
    classes = labels.shape[1]
    group = classes // NY
    held = group + (-group) % 8
    slice_width = width // (NY * NL)
    half = rows // 2

    ids = sample_ids.reshape(NC, rows // NC)
    ids = jnp.where(c == 1, ids[::-1], ids)
    picked = jnp.take(fisher, ids.reshape(rows), axis=0, mode="clip")

    by_slice = [
        lax.dynamic_slice_in_dim(picked, (2 * j + l) * slice_width, slice_width, 1) for j in range(NY)
    ]
    by_other = [
        lax.dynamic_slice_in_dim(picked, (2 * j + 1 - l) * slice_width, slice_width, 1) for j in range(NY)
    ]
    per_part = NY // PARTS
    blocks = []

    def along_y(wide):
        before = turn(wide, "y", 1)
        after = turn(wide, "y", -1)
        far = jnp.concatenate([turn(before[:half], "y", 1), turn(after[half:], "y", -1)], axis=0)
        return [(0.5 * v).astype(jnp.bfloat16) for v in (wide, before, far, after)]

    for k in range(PARTS):
        with jax.named_scope("rows_of_all_blocks"):
            mine = jnp.concatenate(by_slice[k * per_part:(k + 1) * per_part], axis=1)
            other = jnp.concatenate(by_other[k * per_part:(k + 1) * per_part], axis=1)
            wide = 2.0 * mine.astype(jnp.float32)
            partner = turn(2.0 * other.astype(jnp.float32), "l", 1)
            mine = along_y(wide)
            partner = along_y(partner)
            first = [jnp.where(l == 0, a, b) for a, b in zip(mine, partner)]
            second = [jnp.where(l == 0, b, a) for a, b in zip(mine, partner)]
            pieces = []
            for side in (first, second):
                slots = [v.reshape(NC, 1, NZ * NH, 1, PIECE, -1) for v in side]
                pieces.append(jnp.concatenate(slots, axis=3))
            blocks.append(jnp.concatenate(pieces, axis=1).reshape(NL * NY * rows, -1))

    with jax.named_scope("margins"):
        partial = jnp.dot(picked, weights, preferred_element_type=jnp.float32)
        partial = partial[:half] + turn(partial[half:], "c", 1)
        summed = lax.all_to_all(partial, ("z", "h"), 0, 0, tiled=True)
        summed = jnp.sum(summed.reshape(NZ * NH, PIECE, classes), axis=0)
        own_labels = lax.dynamic_slice_in_dim(labels, ((c * NZ + z) * NH + h) * PIECE, PIECE, 0)
        label_sign = 2.0 * own_labels.astype(jnp.float32) - 1.0
        fit = jax.nn.sigmoid(label_sign * summed)
        loss_weight = PENALTY * (fit - 1.0) * label_sign
        curv = PENALTY * fit * (1.0 - fit)
        both = jnp.stack([loss_weight, curv]).reshape(2, PIECE, NY, group).transpose(2, 0, 3, 1)
        both = jnp.pad(both, ((0, 0), (0, 0), (0, held - group), (0, 0)))
        slots = []
        for k in range(NY):
            part = lax.dynamic_index_in_dim(both, (y + k) % NY, 0, keepdims=False)
            slots.append(part if k == 0 else turn(part, "y", k))
        both = jnp.concatenate(slots, axis=2)
        loss_share, curv_share = both[0], both[1]

    def spread(share):
        high = share.shape[0]
        sent = jnp.broadcast_to(share[None], (TEAM, high, 128)).reshape(TEAM * high, 128)
        near = lax.all_to_all(sent, GROUP, 0, 0, tiled=True)
        far = turn(near, "c", 1)
        pair = jnp.stack([near, far]).reshape(NC * TEAM, high, 128)
        whole = pair[:, :held].transpose(1, 0, 2).reshape(held, NC * TEAM * 128)
        return whole, jnp.sum(pair[:, held:], axis=0)

    def reduce(partial, tile):
        mid = partial.shape[1] // 2
        near = partial[:, :mid] + turn(partial[:, mid:], "c", 1)
        tile = tile + turn(tile, "c", 1)
        near = near.reshape(held, TEAM, 128).transpose(1, 0, 2)
        sent = jnp.concatenate([near, jnp.broadcast_to(tile[None], (TEAM, 8, 128))], axis=1)
        got = lax.all_to_all(sent.reshape(TEAM * (held + 8), 128), GROUP, 0, 0, tiled=True)
        total = jnp.sum(got.reshape(TEAM, held + 8, 128), axis=0)
        return total[:held], total[held:]

    with jax.named_scope("loss_spread"):
        loss_all, _ = spread(loss_share)

    own_weights = lax.dynamic_slice_in_dim(weights, y * group, group, 1).astype(jnp.float32).T
    own_weights = jnp.pad(own_weights, ((0, held - group), (0, 0)))
    own_weights = own_weights.reshape(held, NY, NL, slice_width)
    own_weights = lax.dynamic_index_in_dim(own_weights, l, 2, keepdims=False).reshape(held, NY * slice_width)
    part_width = per_part * slice_width

    residual = []
    partial, norm = 0.0, 0.0
    split = halves(loss_all)
    for k in range(PARTS):
        with jax.named_scope("gradient"):
            value = -(own_weights[:, k * part_width:(k + 1) * part_width] + product(split, blocks[k], 0))
            residual.append(value)
            norm = norm + jnp.sum(value * value, axis=1)
            partial = partial + product(halves(value), blocks[k], 1)

    step = [0.0] * PARTS
    direction = swing = norm_now = None
    for iteration in range(ITERS):
        with jax.named_scope("sum_over_features"):
            mapped, tile = reduce(partial, to_tile([norm]))
            norm_next = from_tile(tile, 0, held)
        if iteration == 0:
            direction, swing = list(residual), mapped
        else:
            beta = (norm_next / norm_now)[:, None]
            direction = [r + beta * d for r, d in zip(residual, direction)]
            swing = mapped + beta * swing
        norm_now = norm_next
        with jax.named_scope("spread_scaled"):
            scaled = curv_share * swing
            curved = jnp.sum(scaled * swing, axis=1)
            plain = sum(jnp.sum(d * d, axis=1) for d in direction)
            tile = to_tile([curved, plain])
            scaled_all, tile = spread(jnp.concatenate([scaled, tile], axis=0))
            alpha = (norm_now / (from_tile(tile, 1, held) + from_tile(tile, 0, held)))[:, None]
        step = [n + alpha * d for n, d in zip(step, direction)]
        last = iteration == ITERS - 1
        partial, norm = 0.0, 0.0
        split = halves(scaled_all)
        for k in range(PARTS):
            with jax.named_scope("image"):
                image = direction[k] + product(split, blocks[k], 0)
                residual[k] = residual[k] - alpha * image
                if not last:
                    norm = norm + jnp.sum(residual[k] * residual[k], axis=1)
                    partial = partial + product(halves(residual[k]), blocks[k], 1)

    def place_out(parts):
        stacked = jnp.concatenate(parts, axis=1).reshape(held, NY, slice_width).transpose(1, 0, 2)
        ordered = lax.all_to_all(stacked, "y", 0, 0, tiled=True)
        return ordered[:, :group].reshape(classes, slice_width).T[None]

    with jax.named_scope("outputs"):
        return place_out(step), place_out(residual)


def solution(mesh):
    fine = Mesh(mesh.devices.reshape(SIZES), AXES)
    dp, feat = ("y", "l"), ("z", "h", "c")
    return jax.shard_map(
        shards,
        mesh=fine,
        in_specs=(P(dp, feat), P(dp), P(dp, None), P(feat, None)),
        out_specs=(P(feat, dp, None), P(feat, dp, None)),
        check_vma=False,
    )
```

```python
import functools

import jax
import jax.numpy as jnp
from jax import lax
from jax.experimental import pallas as pl
from jax.experimental.pallas import tpu as pltpu
from jax.sharding import Mesh, PartitionSpec as P

ITERS = 3
PENALTY = 8.0
SIZES = (4, 2, 4, 2, 2)
AXES = ("y", "l", "z", "h", "c")
NY, NL, NZ, NH, NC = SIZES
GROUP = ("l", "z", "h")
TEAM = NL * NZ * NH
PIECE = 32
PARTS = 2


def turn(value, axis, by):
    count = SIZES[AXES.index(axis)]
    return lax.ppermute(value, axis, [(i, (i + by) % count) for i in range(count)])


def halves(value):
    high = lax.reduce_precision(value, 8, 7)
    return jnp.concatenate([high.astype(jnp.bfloat16), (value - high).astype(jnp.bfloat16)], axis=0)


def product(both, matrix, dim):
    out = lax.dot_general(both, matrix, (((1,), (dim,)), ((), ())), preferred_element_type=jnp.float32)
    count = both.shape[0] // 2
    return out[:count] + out[count:]


def to_tile(vectors):
    tile = jnp.concatenate([jnp.pad(v, (0, 256 - v.shape[0])).reshape(2, 128) for v in vectors], axis=0)
    return jnp.pad(tile, ((0, 8 - tile.shape[0]), (0, 0)))


def from_tile(tile, place, count):
    return tile[2 * place:2 * place + 2].reshape(256)[:count]


def after(value, *others):
    return lax.optimization_barrier((value,) + others)[0]


def pick_kernel(side_ref, ids_ref, fisher_ref, wide_ref, picked_ref, chosen):
    @pl.when(pl.program_id(0) == 0)
    def _():
        places = lax.broadcasted_iota(jnp.int32, chosen.shape, 0)
        chosen[...] = jnp.where(ids_ref[...] == places, 1.0, 0.0).T.astype(jnp.bfloat16)

    rows = jnp.dot(chosen[...], fisher_ref[...], preferred_element_type=jnp.float32)
    picked_ref[...] = rows.astype(jnp.bfloat16)
    wide_ref[0, 0] = 2.0 * rows


def pick(fisher, ids, l, slice_width):
    rows, width = fisher.shape
    per_part = NY // PARTS

    def column(s, side):
        return 2 * (s % NY) + (side[0] + s // NY) % 2

    return pl.pallas_call(
        pick_kernel,
        grid_spec=pltpu.PrefetchScalarGridSpec(
            num_scalar_prefetch=1,
            grid=(NY * NL,),
            in_specs=[
                pl.BlockSpec((1, rows), lambda s, side: (0, 0)),
                pl.BlockSpec((rows, slice_width), lambda s, side: (0, column(s, side))),
            ],
            out_specs=[
                pl.BlockSpec(
                    (1, 1, rows, slice_width),
                    lambda s, side: (s // NY, (s % NY) // per_part, 0, (s % NY) % per_part),
                ),
                pl.BlockSpec((rows, slice_width), lambda s, side: (0, column(s, side))),
            ],
            scratch_shapes=[pltpu.VMEM((rows, rows), jnp.bfloat16)],
        ),
        out_shape=[
            jax.ShapeDtypeStruct((NL, PARTS, rows, per_part * slice_width), jnp.float32),
            jax.ShapeDtypeStruct((rows, width), jnp.bfloat16),
        ],
        cost_estimate=pl.CostEstimate(
            flops=2 * rows * rows * width, bytes_accessed=8 * rows * width, transcendentals=0
        ),
        name="pick",
    )(l.reshape(1), ids, fisher)


def place_kernel(group, parts_ref, *out_refs):
    for i, out_ref in enumerate(out_refs):
        for g in range(NY):
            out_ref[g * group:(g + 1) * group, 0, :] = parts_ref[g, i, :group]


def place(parts, group):
    shape = jax.ShapeDtypeStruct((NY * group, 1, parts.shape[3]), jnp.float32)
    outs = pl.pallas_call(functools.partial(place_kernel, group), out_shape=(shape, shape), name="place")(parts)
    return tuple(v.transpose(1, 2, 0) for v in outs)


def shards(fisher, sample_ids, labels, weights):
    y, l, z, h, c = [lax.axis_index(a) for a in AXES]
    rows, width = fisher.shape
    classes = labels.shape[1]
    group = classes // NY
    held = group + (-group) % 8
    slice_width = width // (NY * NL)
    half = rows // 2

    ids = sample_ids.reshape(1, rows)
    ids = jnp.where(c == 1, jnp.concatenate([ids[:, half:], ids[:, :half]], axis=1), ids)
    wide, picked = pick(fisher, ids, l, slice_width)

    per_part = NY // PARTS
    part_width = per_part * slice_width

    def both_ways(value):
        return turn(value, "y", 1), turn(value, "y", -1)

    with jax.named_scope("rows_own"):
        mine = [wide[0, k] for k in range(PARTS)]
        first = both_ways(mine[0])

    with jax.named_scope("margins"):
        partial = jnp.dot(picked, weights, preferred_element_type=jnp.float32)
        partial = partial[:half] + turn(partial[half:], "c", 1)
        summed = lax.all_to_all(partial, ("z", "h"), 0, 0, tiled=True)
        summed = jnp.sum(summed.reshape(NZ * NH, PIECE, classes), axis=0)
        own_labels = lax.dynamic_slice_in_dim(after(labels, partial), ((c * NZ + z) * NH + h) * PIECE, PIECE, 0)
        label_sign = 2.0 * own_labels.astype(jnp.float32) - 1.0
        fit = jax.nn.sigmoid(label_sign * summed)
        loss_weight = PENALTY * (fit - 1.0) * label_sign
        curv = PENALTY * fit * (1.0 - fit)
        both = jnp.concatenate([loss_weight, curv], axis=0)
        slots = []
        for k in range(NY):
            part = lax.dynamic_slice_in_dim(both, (y + k) % NY * group, group, 1)
            slots.append(part if k == 0 else turn(part, "y", k))
        both = jnp.stack(slots).reshape(NY, 2, PIECE, group).transpose(1, 3, 0, 2).reshape(2, group, NY * PIECE)
        both = jnp.pad(both, ((0, 0), (0, held - group), (0, 0)))
        loss_share, curv_share = both[0], both[1]

    with jax.named_scope("rows_exchanged"):
        theirs = [turn(after(wide[1, 0], summed), "l", 1)]
        theirs.append(turn(after(wide[1, 1], theirs[0]), "l", 1))
        second = both_ways(after(mine[1], loss_weight))
        mine, own_weights = lax.optimization_barrier((mine, weights, loss_weight))[:2]

    def spread(share):
        high = share.shape[0]
        sent = jnp.broadcast_to(share[None], (TEAM, high, 128)).reshape(TEAM * high, 128)
        return lax.all_to_all(sent, GROUP, 0, 0, tiled=True)

    def spread_cores(near):
        high = near.shape[0] // TEAM
        far = turn(near, "c", 1)
        pair = jnp.stack([near, far]).reshape(NC * TEAM, high, 128)
        kept = high - 8
        whole = pair[:, :kept].transpose(1, 0, 2).reshape(kept, NC * TEAM * 128)
        return whole, jnp.sum(pair[:, kept:], axis=0)

    def reduce(partial, tile):
        count = partial.shape[0]
        mid = partial.shape[1] // 2
        near = partial[:, :mid] + turn(partial[:, mid:], "c", 1)
        tile = tile + turn(tile, "c", 1)
        near = near.reshape(count, TEAM, 128).transpose(1, 0, 2)
        sent = jnp.concatenate([near, jnp.broadcast_to(tile[None], (TEAM, 8, 128))], axis=1)
        got = lax.all_to_all(sent.reshape(TEAM * (count + 8), 128), GROUP, 0, 0, tiled=True)
        total = jnp.sum(got.reshape(TEAM, count + 8, 128), axis=0)
        return total[:count], total[count:]

    with jax.named_scope("rows_along_y"):
        far_own = [turn(first[0], "y", 1), turn(second[1], "y", -1)]
        near = spread(loss_share)
        third = both_ways(theirs[0])
        fourth = both_ways(theirs[1])
        far = turn(after(near, theirs[1]), "c", 1)
        far_their = [turn(third[0], "y", 1), turn(fourth[1], "y", -1)]
        blocks = []
        for k in range(PARTS):
            sides = [
                [(0.5 * v).astype(jnp.bfloat16).reshape(NC, NZ * NH, PIECE, part_width) for v in side]
                for side in (
                    (mine[k], (first, second)[k][0], far_own[k], (first, second)[k][1]),
                    (theirs[k], (third, fourth)[k][0], far_their[k], (third, fourth)[k][1]),
                )
            ]
            sides = [jnp.stack(side, axis=2) for side in sides]
            ordered = [jnp.where(l == 0, sides[0], sides[1]), jnp.where(l == 0, sides[1], sides[0])]
            blocks.append(jnp.stack(ordered, axis=1).reshape(NL * NY * rows, part_width))

    with jax.named_scope("loss_spread"):
        pair = jnp.stack([near, far]).reshape(NC * TEAM, held, 128)
        loss_all = pair.transpose(1, 0, 2).reshape(held, NC * TEAM * 128)

    own_weights = lax.dynamic_slice_in_dim(own_weights, y * group, group, 1).astype(jnp.float32).T
    own_weights = jnp.pad(own_weights, ((0, held - group), (0, 0)))
    own_weights = own_weights.reshape(held, NY, NL, slice_width)
    own_weights = lax.dynamic_index_in_dim(own_weights, l, 2, keepdims=False).reshape(held, NY * slice_width)

    with jax.named_scope("gradient"):
        residual, norm, partial = [], 0.0, 0.0
        split = halves(loss_all)
        for k in range(PARTS):
            value = -(own_weights[:, k * part_width:(k + 1) * part_width] + product(split, blocks[k], 0))
            residual.append(value)
            norm = norm + jnp.sum(value * value, axis=1)
            partial = partial + product(halves(value), blocks[k], 1)

    step = [0.0] * PARTS
    direction = swing = norm_now = None
    for iteration in range(ITERS):
        with jax.named_scope("sum_over_features"):
            mapped, tile = reduce(partial, to_tile([norm]))
            norm_next = from_tile(tile, 0, held)
        if iteration == 0:
            direction, swing = list(residual), mapped
        else:
            beta = (norm_next / norm_now)[:, None]
            direction = [r + beta * d for r, d in zip(residual, direction)]
            swing = mapped + beta * swing
        norm_now = norm_next
        with jax.named_scope("spread_scaled"):
            scaled = curv_share * swing
            curved = jnp.sum(scaled * swing, axis=1)
            plain = sum(jnp.sum(d * d, axis=1) for d in direction)
            tile = to_tile([curved, plain])
            scaled_all, tile = spread_cores(spread(jnp.concatenate([scaled, tile], axis=0)))
            alpha = (norm_now / (from_tile(tile, 1, held) + from_tile(tile, 0, held)))[:, None]
        step = [n + alpha * d for n, d in zip(step, direction)]
        last = iteration == ITERS - 1
        partial, norm = 0.0, 0.0
        split = halves(scaled_all)
        for k in range(PARTS):
            with jax.named_scope("image"):
                image = direction[k] + product(split, blocks[k], 0)
                residual[k] = residual[k] - alpha * image
                if not last:
                    norm = norm + jnp.sum(residual[k] * residual[k], axis=1)
                    partial = partial + product(halves(residual[k]), blocks[k], 1)

    with jax.named_scope("outputs"):
        by_owner = [
            v[:, j * slice_width:(j + 1) * slice_width]
            for a, b in zip(step, residual) for j in range(per_part) for v in (a, b)
        ]
        stacked = jnp.stack(by_owner).reshape(NY, 2 * held, slice_width)
        ordered = lax.all_to_all(stacked, "y", 0, 0, tiled=True).reshape(NY, 2, held, slice_width)
        return place(ordered, group)


def solution(mesh):
    fine = Mesh(mesh.devices.reshape(SIZES), AXES)
    dp, feat = ("y", "l"), ("z", "h", "c")
    return jax.shard_map(
        shards,
        mesh=fine,
        in_specs=(P(dp, feat), P(dp), P(dp, None), P(feat, None)),
        out_specs=(P(feat, dp, None), P(feat, dp, None)),
        check_vma=False,
    )
```

```python
import functools

import jax
import jax.numpy as jnp
from jax import lax
from jax.experimental import pallas as pl
from jax.experimental.pallas import tpu as pltpu
from jax.sharding import Mesh, PartitionSpec as P

ITERS = 3
PENALTY = 8.0
SIZES = (4, 2, 4, 2, 2)
AXES = ("y", "l", "z", "h", "c")
NY, NL, NZ, NH, NC = SIZES
GROUP = ("l", "z", "h")
TEAM = NL * NZ * NH
PIECE = 32
PARTS = 2


def turn(value, axis, by):
    count = SIZES[AXES.index(axis)]
    return lax.ppermute(value, axis, [(i, (i + by) % count) for i in range(count)])


def halves(value):
    high = lax.reduce_precision(value, 8, 7)
    return jnp.concatenate([high.astype(jnp.bfloat16), (value - high).astype(jnp.bfloat16)], axis=0)


def times(both, matrix, dim):
    return lax.dot_general(both, matrix, (((1,), (dim,)), ((), ())), preferred_element_type=jnp.float32)


def folded(both):
    count = both.shape[0] // 2
    return both[:count] + both[count:]


def to_tile(vectors):
    tile = jnp.concatenate([jnp.pad(v, (0, 256 - v.shape[0])).reshape(2, 128) for v in vectors], axis=0)
    return jnp.pad(tile, ((0, 8 - tile.shape[0]), (0, 0)))


def from_tile(tile, place, count):
    return tile[2 * place:2 * place + 2].reshape(256)[:count]


def after(value, *others):
    return lax.optimization_barrier((value,) + others)[0]


def pick_kernel(at_ref, ids_ref, fisher_ref, *refs):
    *wide_refs, picked_ref, chosen = refs
    step = pl.program_id(0)

    @pl.when(step == 0)
    def _():
        ids = ids_ref[...]
        half = ids.shape[1] // 2
        ids = jnp.where(at_ref[0] % NC == 1, jnp.concatenate([ids[:, half:], ids[:, :half]], axis=1), ids)
        places = lax.broadcasted_iota(jnp.int32, chosen.shape, 0)
        chosen[...] = jnp.where(ids == places, 1.0, 0.0).T.astype(jnp.bfloat16)

    rows = jnp.dot(chosen[...], fisher_ref[...], preferred_element_type=jnp.float32)
    picked_ref[...] = rows.astype(jnp.bfloat16)
    for k, wide_ref in enumerate(wide_refs):
        @pl.when(step // (NY // PARTS) == k)
        def _():
            wide_ref[...] = 2.0 * rows


def pick(fisher, ids, at, slice_width):
    rows, width = fisher.shape
    per_part = NY // PARTS

    def column(s, at):
        return 2 * (s % NY) + (at[0] // NC + s // NY) % NL

    def part_spec(k):
        return pl.BlockSpec((rows, slice_width), lambda s, at: (0, jnp.clip(s - k * per_part, 0, per_part - 1)))

    *wide, picked = pl.pallas_call(
        pick_kernel,
        grid_spec=pltpu.PrefetchScalarGridSpec(
            num_scalar_prefetch=1,
            grid=(NY * NL,),
            in_specs=[
                pl.BlockSpec((1, rows), lambda s, at: (0, 0)),
                pl.BlockSpec((rows, slice_width), lambda s, at: (0, column(s, at))),
            ],
            out_specs=[part_spec(k) for k in range(NL * PARTS)]
            + [pl.BlockSpec((rows, slice_width), lambda s, at: (0, column(s, at)))],
            scratch_shapes=[pltpu.VMEM((rows, rows), jnp.bfloat16)],
        ),
        out_shape=[jax.ShapeDtypeStruct((rows, per_part * slice_width), jnp.float32)] * (NL * PARTS)
        + [jax.ShapeDtypeStruct((rows, width), jnp.bfloat16)],
        cost_estimate=pl.CostEstimate(
            flops=2 * rows * rows * width, bytes_accessed=8 * rows * width, transcendentals=0
        ),
        name="pick",
    )(at, ids, fisher)
    return wide[:PARTS], wide[PARTS:], picked


def place_kernel(group, parts_ref, *out_refs):
    for i, out_ref in enumerate(out_refs):
        for g in range(NY):
            out_ref[g * group:(g + 1) * group, 0, :] = parts_ref[g, i, :group]


def place(parts, group):
    shape = jax.ShapeDtypeStruct((NY * group, 1, parts.shape[3]), jnp.float32)
    outs = pl.pallas_call(functools.partial(place_kernel, group), out_shape=(shape, shape), name="place")(parts)
    return tuple(v.transpose(1, 2, 0) for v in outs)


def shards(fisher, sample_ids, labels, weights):
    y, l, z, h, c = [lax.axis_index(a) for a in AXES]
    rows, width = fisher.shape
    classes = labels.shape[1]
    group = classes // NY
    held = group + (-group) % 8
    slice_width = width // (NY * NL)
    half = rows // 2

    mine, other, picked = pick(fisher, sample_ids.reshape(1, rows), (l * NC + c).reshape(1), slice_width)

    per_part = NY // PARTS
    part_width = per_part * slice_width

    def both_ways(value):
        return turn(value, "y", 1), turn(value, "y", -1)

    with jax.named_scope("rows_own"):
        first = both_ways(mine[0])

    with jax.named_scope("margins"):
        partial = jnp.dot(picked, weights, preferred_element_type=jnp.float32)
        partial = partial[:half] + turn(partial[half:], "c", 1)
        summed = lax.all_to_all(partial, ("z", "h"), 0, 0, tiled=True)
        summed = jnp.sum(summed.reshape(NZ * NH, PIECE, classes), axis=0)
        own_labels = lax.dynamic_slice_in_dim(after(labels, partial), ((c * NZ + z) * NH + h) * PIECE, PIECE, 0)
        label_sign = 2.0 * own_labels.astype(jnp.float32) - 1.0
        fit = jax.nn.sigmoid(label_sign * summed)
        loss_weight = PENALTY * (fit - 1.0) * label_sign
        curv = PENALTY * fit * (1.0 - fit)
        both = jnp.concatenate([loss_weight, curv], axis=0)
        slots = []
        for k in range(NY):
            part = lax.dynamic_slice_in_dim(both, (y + k) % NY * group, group, 1)
            slots.append(part if k == 0 else turn(part, "y", k))
        both = jnp.stack(slots).reshape(NY, 2, PIECE, group).transpose(1, 3, 0, 2).reshape(2, group, NY * PIECE)
        both = jnp.pad(both, ((0, 0), (0, held - group), (0, 0)))
        loss_share, curv_share = both[0], both[1]

    with jax.named_scope("rows_exchanged"):
        theirs = [turn(after(other[0], summed), "l", 1)]
        theirs.append(turn(after(other[1], theirs[0]), "l", 1))
        second = turn(after(mine[1], loss_weight), "y", 1), turn(after(mine[1], first[1]), "y", -1)
        own_weights = after(weights, loss_weight)

    def spread(share):
        count = share.shape[0]
        sent = jnp.broadcast_to(share[None], (TEAM, count, 128)).reshape(TEAM * count, 128)
        return lax.all_to_all(sent, GROUP, 0, 0, tiled=True)

    def opened(shares):
        shares = shares.reshape(TEAM, -1, 128)
        whole = shares[:, :held].transpose(1, 0, 2).reshape(held, TEAM * 128)
        return halves(whole), jnp.sum(shares[:, held:], axis=0)

    def back(near, far, k):
        return folded(times(near, blocks[k][0], 0) + times(far, blocks[k][1], 0))

    def reduce(residual, tile):
        split = [halves(v) for v in residual]
        far = turn(folded(sum(times(v, blocks[k][1], 1) for k, v in enumerate(split))), "c", 1)
        near = folded(sum(times(v, blocks[k][0], 1) for k, v in enumerate(split))) + far
        tile = tile + turn(tile, "c", 1)
        near = near.reshape(held, TEAM, 128).transpose(1, 0, 2)
        sent = jnp.concatenate([near, jnp.broadcast_to(tile[None], (TEAM, 8, 128))], axis=1)
        got = lax.all_to_all(sent.reshape(TEAM * (held + 8), 128), GROUP, 0, 0, tiled=True)
        total = jnp.sum(got.reshape(TEAM, held + 8, 128), axis=0)
        return total[:held], total[held:]

    with jax.named_scope("rows_along_y"):
        far_own = [turn(first[0], "y", 1), turn(second[1], "y", -1)]
        near = spread(after(loss_share, theirs[0]))
        third = both_ways(theirs[0])
        fourth = both_ways(theirs[1])
        far = turn(after(near, theirs[1]), "c", 1)
        far_their = [turn(third[0], "y", 1), turn(fourth[1], "y", -1)]
        blocks = []
        for k in range(PARTS):
            sides = [
                [(0.5 * v).astype(jnp.bfloat16).reshape(NC, NZ * NH, PIECE, part_width) for v in side]
                for side in (
                    (mine[k], (first, second)[k][0], far_own[k], (first, second)[k][1]),
                    (theirs[k], (third, fourth)[k][0], far_their[k], (third, fourth)[k][1]),
                )
            ]
            of_cores = []
            for core in range(NC):
                pair = [jnp.stack([v[core] for v in side], axis=1) for side in sides]
                pair = [jnp.where(l == 0, pair[0], pair[1]), jnp.where(l == 0, pair[1], pair[0])]
                of_cores.append(jnp.stack(pair).reshape(NL * NY * half, part_width))
            blocks.append(of_cores)

    own_weights = lax.dynamic_slice_in_dim(own_weights, y * group, group, 1).astype(jnp.float32).T
    own_weights = jnp.pad(own_weights, ((0, held - group), (0, 0)))
    own_weights = own_weights.reshape(held, NY, NL, slice_width)
    own_weights = lax.dynamic_index_in_dim(own_weights, l, 2, keepdims=False).reshape(held, NY * slice_width)

    with jax.named_scope("gradient"):
        near, far = opened(near)[0], opened(far)[0]
        residual = [
            -(own_weights[:, k * part_width:(k + 1) * part_width] + back(near, far, k)) for k in range(PARTS)
        ]

    step = [0.0] * PARTS
    direction = swing = norm_now = None
    for iteration in range(ITERS):
        with jax.named_scope("sum_over_features"):
            norm = sum(jnp.sum(v * v, axis=1) for v in residual)
            mapped, tile = reduce(residual, to_tile([norm]))
            norm_next = from_tile(tile, 0, held)
        if iteration == 0:
            direction, swing = residual, mapped
        else:
            beta = (norm_next / norm_now)[:, None]
            direction = [r + beta * d for r, d in zip(residual, direction)]
            swing = mapped + beta * swing
        norm_now = norm_next
        with jax.named_scope("spread_scaled"):
            scaled = curv_share * swing
            curved = jnp.sum(scaled * swing, axis=1)
            plain = sum(jnp.sum(d * d, axis=1) for d in direction)
            near = spread(jnp.concatenate([scaled, to_tile([curved, plain])], axis=0))
            (near, tile), (far, far_tile) = opened(near), opened(turn(near, "c", 1))
            tile = tile + far_tile
            alpha = (norm_now / (from_tile(tile, 1, held) + from_tile(tile, 0, held)))[:, None]
        with jax.named_scope("image"):
            step = [n + alpha * d for n, d in zip(step, direction)]
            residual = [r - alpha * (d + back(near, far, k)) for k, (r, d) in enumerate(zip(residual, direction))]

    with jax.named_scope("outputs"):
        by_owner = [
            v[:, j * slice_width:(j + 1) * slice_width]
            for a, b in zip(step, residual) for j in range(per_part) for v in (a, b)
        ]
        stacked = jnp.stack(by_owner).reshape(NY, 2 * held, slice_width)
        ordered = lax.all_to_all(stacked, "y", 0, 0, tiled=True).reshape(NY, 2, held, slice_width)
        return place(ordered, group)


def solution(mesh):
    fine = Mesh(mesh.devices.reshape(SIZES), AXES)
    dp, feat = ("y", "l"), ("z", "h", "c")
    return jax.shard_map(
        shards,
        mesh=fine,
        in_specs=(P(dp, feat), P(dp), P(dp, None), P(feat, None)),
        out_specs=(P(feat, dp, None), P(feat, dp, None)),
        check_vma=False,
    )
```

```python
import functools

import jax
import jax.numpy as jnp
from jax import lax
from jax.experimental import pallas as pl
from jax.experimental.pallas import tpu as pltpu
from jax.sharding import Mesh, PartitionSpec as P

ITERS = 3
PENALTY = 8.0
SIZES = (4, 2, 4, 2, 2)
AXES = ("y", "l", "z", "h", "c")
NY, NL, NZ, NH, NC = SIZES
GROUP = ("l", "z", "h")
TEAM = NL * NZ * NH
PIECE = 32
PARTS = 2


def turn(value, axis, by):
    count = SIZES[AXES.index(axis)]
    return lax.ppermute(value, axis, [(i, (i + by) % count) for i in range(count)])


def halves(value):
    high = lax.reduce_precision(value, 8, 7)
    return jnp.concatenate([high.astype(jnp.bfloat16), (value - high).astype(jnp.bfloat16)], axis=0)


def times(both, matrix, dim):
    return lax.dot_general(both, matrix, (((1,), (dim,)), ((), ())), preferred_element_type=jnp.float32)


def folded(both):
    count = both.shape[0] // 2
    return both[:count] + both[count:]


def to_tile(vectors):
    tile = jnp.concatenate([jnp.pad(v, (0, 256 - v.shape[0])).reshape(2, 128) for v in vectors], axis=0)
    return jnp.pad(tile, ((0, 8 - tile.shape[0]), (0, 0)))


def from_tile(tile, place, count):
    return tile[2 * place:2 * place + 2].reshape(256)[:count]


def after(value, *others):
    return lax.optimization_barrier((value,) + others)[0]


def pick_kernel(slice_width, at_ref, ids_ref, fisher_ref, *refs):
    *wide_refs, picked_ref = refs
    rows = fisher_ref.shape[0]
    half = rows // 2
    ids = ids_ref[...]
    ids = jnp.where(at_ref[0] % NC == 1, jnp.concatenate([ids[:, half:], ids[:, :half]], axis=1), ids)
    places = lax.broadcasted_iota(jnp.int32, (rows, rows), 0)
    chosen = jnp.where(ids == places, 1.0, 0.0).T.astype(jnp.bfloat16)
    for s in range(NL * NY):
        side, j = s // NY, s % NY
        first = pl.multiple_of((2 * j + (at_ref[0] // NC + side) % NL) * slice_width, slice_width)
        part = jnp.dot(chosen, fisher_ref[:, pl.ds(first, slice_width)], preferred_element_type=jnp.float32)
        picked_ref[:, pl.ds(first, slice_width)] = part.astype(jnp.bfloat16)
        per_part = NY // PARTS
        columns = slice(j % per_part * slice_width, (j % per_part + 1) * slice_width)
        wide_refs[s // per_part][:, columns] = 2.0 * part


def pick(fisher, ids, at, slice_width):
    rows, width = fisher.shape
    vmem = pl.BlockSpec(memory_space=pltpu.VMEM)
    *wide, picked = pl.pallas_call(
        functools.partial(pick_kernel, slice_width),
        in_specs=[pl.BlockSpec(memory_space=pltpu.SMEM), vmem, vmem],
        out_specs=[vmem] * (NL * PARTS + 1),
        out_shape=[pltpu.VMEM((rows, NY // PARTS * slice_width), jnp.float32)] * (NL * PARTS)
        + [pltpu.VMEM((rows, width), jnp.bfloat16)],
        compiler_params=pltpu.CompilerParams(vmem_limit_bytes=24 * 2**20),
        cost_estimate=pl.CostEstimate(
            flops=2 * rows * rows * width, bytes_accessed=8 * rows * width, transcendentals=0
        ),
        name="pick",
    )(at, ids, fisher)
    return wide[:PARTS], wide[PARTS:], picked


def assemble_kernel(l_ref, *refs):
    block_refs, out_refs = refs[:-NC], refs[-NC:]
    team_half = NZ * NH
    for i, block_ref in enumerate(block_refs):
        side, slot = i // NY, i % NY
        first = pl.multiple_of((l_ref[0] + side) % NL * (team_half * NY * PIECE), team_half * NY * PIECE)
        for core, out_ref in enumerate(out_refs):
            for chip in range(team_half):
                piece = block_ref[pl.ds((core * team_half + chip) * PIECE, PIECE), :]
                out_ref[pl.ds(first + (chip * NY + slot) * PIECE, PIECE), :] = piece


def assemble(mine, theirs, l):
    rows, width = mine[0].shape
    vmem = pl.BlockSpec(memory_space=pltpu.VMEM)
    return pl.pallas_call(
        assemble_kernel,
        in_specs=[pl.BlockSpec(memory_space=pltpu.SMEM)] + [vmem] * (NL * NY),
        out_specs=[vmem] * NC,
        out_shape=[pltpu.VMEM((NL * NY * rows // NC, width), jnp.bfloat16)] * NC,
        compiler_params=pltpu.CompilerParams(vmem_limit_bytes=24 * 2**20),
        name="assemble",
    )(l.reshape(1), *mine, *theirs)


def place_kernel(group, parts_ref, *out_refs):
    for i, out_ref in enumerate(out_refs):
        for g in range(NY):
            out_ref[g * group:(g + 1) * group, 0, :] = parts_ref[g, i, :group]


def place(parts, group):
    shape = jax.ShapeDtypeStruct((NY * group, 1, parts.shape[3]), jnp.float32)
    outs = pl.pallas_call(functools.partial(place_kernel, group), out_shape=(shape, shape), name="place")(parts)
    return tuple(v.transpose(1, 2, 0) for v in outs)


def shards(fisher, sample_ids, labels, weights):
    y, l, z, h, c = [lax.axis_index(a) for a in AXES]
    rows, width = fisher.shape
    classes = labels.shape[1]
    group = classes // NY
    held = group + (-group) % 8
    slice_width = width // (NY * NL)
    half = rows // 2

    mine, other, picked = pick(fisher, sample_ids.reshape(1, rows), (l * NC + c).reshape(1), slice_width)

    per_part = NY // PARTS
    part_width = per_part * slice_width

    def both_ways(value):
        return turn(value, "y", 1), turn(value, "y", -1)

    with jax.named_scope("rows_own"):
        first = both_ways(mine[0])

    with jax.named_scope("margins"):
        partial = jnp.dot(picked, weights, preferred_element_type=jnp.float32)
        partial = partial[:half] + turn(partial[half:], "c", 1)
        summed = lax.all_to_all(partial, ("z", "h"), 0, 0, tiled=True)
        summed = jnp.sum(summed.reshape(NZ * NH, PIECE, classes), axis=0)
        own_labels = lax.dynamic_slice_in_dim(after(labels, partial), ((c * NZ + z) * NH + h) * PIECE, PIECE, 0)
        label_sign = 2.0 * own_labels.astype(jnp.float32) - 1.0
        fit = jax.nn.sigmoid(label_sign * summed)
        loss_weight = PENALTY * (fit - 1.0) * label_sign
        curv = PENALTY * fit * (1.0 - fit)
        both = jnp.concatenate([loss_weight, curv], axis=0)
        slots = []
        for k in range(NY):
            part = lax.dynamic_slice_in_dim(both, (y + k) % NY * group, group, 1)
            slots.append(part if k == 0 else turn(part, "y", k))
        both = jnp.stack(slots).reshape(NY, 2, PIECE, group).transpose(1, 3, 0, 2).reshape(2, group, NY * PIECE)
        both = jnp.pad(both, ((0, 0), (0, held - group), (0, 0)))
        loss_share, curv_share = both[0], both[1]

    with jax.named_scope("rows_exchanged"):
        theirs = [turn(after(other[0], summed), "l", 1)]
        theirs.append(turn(after(other[1], theirs[0]), "l", 1))
        second = turn(after(mine[1], loss_weight), "y", 1), turn(after(mine[1], first[1]), "y", -1)
        own_weights = after(weights, loss_weight)

    def spread(share):
        count = share.shape[0]
        sent = jnp.broadcast_to(share[None], (TEAM, count, 128)).reshape(TEAM * count, 128)
        return lax.all_to_all(sent, GROUP, 0, 0, tiled=True)

    def opened(shares):
        shares = shares.reshape(TEAM, -1, 128)
        whole = shares[:, :held].transpose(1, 0, 2).reshape(held, TEAM * 128)
        return halves(whole), jnp.sum(shares[:, held:], axis=0)

    def back(near, far, k):
        return folded(times(near, blocks[k][0], 0) + times(far, blocks[k][1], 0))

    def reduce(residual, tile):
        split = [halves(v) for v in residual]
        far = turn(folded(sum(times(v, blocks[k][1], 1) for k, v in enumerate(split))), "c", 1)
        near = folded(sum(times(v, blocks[k][0], 1) for k, v in enumerate(split))) + far
        tile = tile + turn(tile, "c", 1)
        near = near.reshape(held, TEAM, 128).transpose(1, 0, 2)
        sent = jnp.concatenate([near, jnp.broadcast_to(tile[None], (TEAM, 8, 128))], axis=1)
        got = lax.all_to_all(sent.reshape(TEAM * (held + 8), 128), GROUP, 0, 0, tiled=True)
        total = jnp.sum(got.reshape(TEAM, held + 8, 128), axis=0)
        return total[:held], total[held:]

    with jax.named_scope("rows_along_y"):
        far_own = [turn(first[0], "y", 1), turn(second[1], "y", -1)]
        near = spread(after(loss_share, theirs[0]))
        third = both_ways(theirs[0])
        fourth = both_ways(theirs[1])
        far = turn(after(near, theirs[1]), "c", 1)
        far_their = [turn(third[0], "y", 1), turn(fourth[1], "y", -1)]
        blocks = []
        for k in range(PARTS):
            sides = [
                [(0.5 * v).astype(jnp.bfloat16) for v in side]
                for side in (
                    (mine[k], (first, second)[k][0], far_own[k], (first, second)[k][1]),
                    (theirs[k], (third, fourth)[k][0], far_their[k], (third, fourth)[k][1]),
                )
            ]
            blocks.append(assemble(*sides, l))

    own_weights = lax.dynamic_slice_in_dim(own_weights, y * group, group, 1).astype(jnp.float32).T
    own_weights = jnp.pad(own_weights, ((0, held - group), (0, 0)))
    own_weights = own_weights.reshape(held, NY, NL, slice_width)
    own_weights = lax.dynamic_index_in_dim(own_weights, l, 2, keepdims=False).reshape(held, NY * slice_width)

    with jax.named_scope("gradient"):
        near, far = opened(near)[0], opened(far)[0]
        residual = [
            -(own_weights[:, k * part_width:(k + 1) * part_width] + back(near, far, k)) for k in range(PARTS)
        ]

    step = [0.0] * PARTS
    direction = swing = norm_now = None
    for iteration in range(ITERS):
        with jax.named_scope("sum_over_features"):
            norm = sum(jnp.sum(v * v, axis=1) for v in residual)
            mapped, tile = reduce(residual, to_tile([norm]))
            norm_next = from_tile(tile, 0, held)
        if iteration == 0:
            direction, swing = residual, mapped
        else:
            beta = (norm_next / norm_now)[:, None]
            direction = [r + beta * d for r, d in zip(residual, direction)]
            swing = mapped + beta * swing
        norm_now = norm_next
        with jax.named_scope("spread_scaled"):
            scaled = curv_share * swing
            curved = jnp.sum(scaled * swing, axis=1)
            plain = sum(jnp.sum(d * d, axis=1) for d in direction)
            near = spread(jnp.concatenate([scaled, to_tile([curved, plain])], axis=0))
            far = turn(near, "c", 1)
            near, tile = opened(near)
            parts = [times(near, blocks[k][0], 0) for k in range(PARTS)]
            far, *parts = lax.optimization_barrier((far, *parts))
            far, far_tile = opened(far)
            tile = tile + far_tile
            alpha = (norm_now / (from_tile(tile, 1, held) + from_tile(tile, 0, held)))[:, None]
        with jax.named_scope("image"):
            step = [n + alpha * d for n, d in zip(step, direction)]
            image = [d + folded(p + times(far, blocks[k][1], 0)) for k, (d, p) in enumerate(zip(direction, parts))]
            residual = [r - alpha * i for r, i in zip(residual, image)]

    with jax.named_scope("outputs"):
        by_owner = [
            v[:, j * slice_width:(j + 1) * slice_width]
            for a, b in zip(step, residual) for j in range(per_part) for v in (a, b)
        ]
        stacked = jnp.stack(by_owner).reshape(NY, 2 * held, slice_width)
        ordered = lax.all_to_all(stacked, "y", 0, 0, tiled=True).reshape(NY, 2, held, slice_width)
        return place(ordered, group)


def solution(mesh):
    fine = Mesh(mesh.devices.reshape(SIZES), AXES)
    dp, feat = ("y", "l"), ("z", "h", "c")
    return jax.shard_map(
        shards,
        mesh=fine,
        in_specs=(P(dp, feat), P(dp), P(dp, None), P(feat, None)),
        out_specs=(P(feat, dp, None), P(feat, dp, None)),
        check_vma=False,
    )
```

```python
import functools

import jax
import jax.numpy as jnp
from jax import lax
from jax.experimental import pallas as pl
from jax.experimental.pallas import tpu as pltpu
from jax.sharding import Mesh, PartitionSpec as P

ITERS = 3
PENALTY = 8.0
SIZES = (4, 2, 4, 2, 2)
AXES = ("y", "l", "z", "h", "c")
NY, NL, NZ, NH, NC = SIZES
GROUP = ("l", "z", "h")
TEAM = NL * NZ * NH
PIECE = 32
PARTS = 2


def turn(value, axis, by):
    count = SIZES[AXES.index(axis)]
    return lax.ppermute(value, axis, [(i, (i + by) % count) for i in range(count)])


def halves(value):
    high = lax.reduce_precision(value, 8, 7)
    return jnp.concatenate([high.astype(jnp.bfloat16), (value - high).astype(jnp.bfloat16)], axis=0)


def times(both, matrix, dim):
    return lax.dot_general(both, matrix, (((1,), (dim,)), ((), ())), preferred_element_type=jnp.float32)


def folded(both):
    count = both.shape[0] // 2
    return both[:count] + both[count:]


def to_tile(vectors):
    tile = jnp.concatenate([jnp.pad(v, (0, 256 - v.shape[0])).reshape(2, 128) for v in vectors], axis=0)
    return jnp.pad(tile, ((0, 8 - tile.shape[0]), (0, 0)))


def from_tile(tile, place, count):
    return tile[2 * place:2 * place + 2].reshape(256)[:count]


def after(value, *others):
    return lax.optimization_barrier((value,) + others)[0]


def pick_kernel(slice_width, at_ref, ids_ref, fisher_ref, *refs):
    *wide_refs, picked_ref = refs
    rows = fisher_ref.shape[0]
    half = rows // 2
    ids = ids_ref[...]
    ids = jnp.where(at_ref[0] % NC == 1, jnp.concatenate([ids[:, half:], ids[:, :half]], axis=1), ids)
    places = lax.broadcasted_iota(jnp.int32, (rows, rows), 0)
    chosen = jnp.where(ids == places, 1.0, 0.0).T.astype(jnp.bfloat16)
    for s in range(NL * NY):
        side, j = s // NY, s % NY
        first = pl.multiple_of((2 * j + (at_ref[0] // NC + side) % NL) * slice_width, slice_width)
        part = jnp.dot(chosen, fisher_ref[:, pl.ds(first, slice_width)], preferred_element_type=jnp.float32)
        picked_ref[:, pl.ds(first, slice_width)] = part.astype(jnp.bfloat16)
        per_part = NY // PARTS
        columns = slice(j % per_part * slice_width, (j % per_part + 1) * slice_width)
        wide_refs[s // per_part][:, columns] = 2.0 * part


def pick(fisher, ids, at, slice_width):
    rows, width = fisher.shape
    vmem = pl.BlockSpec(memory_space=pltpu.VMEM)
    *wide, picked = pl.pallas_call(
        functools.partial(pick_kernel, slice_width),
        in_specs=[pl.BlockSpec(memory_space=pltpu.SMEM), vmem, vmem],
        out_specs=[vmem] * (NL * PARTS + 1),
        out_shape=[pltpu.VMEM((rows, NY // PARTS * slice_width), jnp.float32)] * (NL * PARTS)
        + [pltpu.VMEM((rows, width), jnp.bfloat16)],
        compiler_params=pltpu.CompilerParams(vmem_limit_bytes=24 * 2**20),
        cost_estimate=pl.CostEstimate(
            flops=2 * rows * rows * width, bytes_accessed=8 * rows * width, transcendentals=0
        ),
        name="pick",
    )(at, ids, fisher)
    return wide[:PARTS], wide[PARTS:], picked


def assemble_kernel(l_ref, *refs):
    block_refs, out_refs = refs[:-NC], refs[-NC:]
    team_half = NZ * NH
    for i, block_ref in enumerate(block_refs):
        side, slot = i // NY, i % NY
        first = pl.multiple_of((l_ref[0] + side) % NL * (team_half * NY * PIECE), team_half * NY * PIECE)
        for core, out_ref in enumerate(out_refs):
            for chip in range(team_half):
                piece = block_ref[pl.ds((core * team_half + chip) * PIECE, PIECE), :]
                out_ref[pl.ds(first + (chip * NY + slot) * PIECE, PIECE), :] = piece


def assemble(mine, theirs, l):
    rows, width = mine[0].shape
    vmem = pl.BlockSpec(memory_space=pltpu.VMEM)
    return pl.pallas_call(
        assemble_kernel,
        in_specs=[pl.BlockSpec(memory_space=pltpu.SMEM)] + [vmem] * (NL * NY),
        out_specs=[vmem] * NC,
        out_shape=[pltpu.VMEM((NL * NY * rows // NC, width), jnp.bfloat16)] * NC,
        compiler_params=pltpu.CompilerParams(vmem_limit_bytes=24 * 2**20),
        name="assemble",
    )(l.reshape(1), *mine, *theirs)


def place_kernel(group, parts_ref, *out_refs):
    for i, out_ref in enumerate(out_refs):
        for g in range(NY):
            out_ref[g * group:(g + 1) * group, 0, :] = parts_ref[g, i, :group]


def place(parts, group):
    shape = jax.ShapeDtypeStruct((NY * group, 1, parts.shape[3]), jnp.float32)
    outs = pl.pallas_call(functools.partial(place_kernel, group), out_shape=(shape, shape), name="place")(parts)
    return tuple(v.transpose(1, 2, 0) for v in outs)


def shards(fisher, sample_ids, labels, weights):
    y, l, z, h, c = [lax.axis_index(a) for a in AXES]
    rows, width = fisher.shape
    classes = labels.shape[1]
    group = classes // NY
    held = group + (-group) % 8
    slice_width = width // (NY * NL)
    half = rows // 2

    mine, other, picked = pick(fisher, sample_ids.reshape(1, rows), (l * NC + c).reshape(1), slice_width)

    per_part = NY // PARTS
    part_width = per_part * slice_width

    def both_ways(value):
        return turn(value, "y", 1), turn(value, "y", -1)

    with jax.named_scope("rows_own"):
        first = both_ways(mine[0])

    with jax.named_scope("margins"):
        partial = jnp.dot(picked, weights, preferred_element_type=jnp.float32)
        partial = partial[:half] + turn(partial[half:], "c", 1)
        summed = lax.all_to_all(partial, ("z", "h"), 0, 0, tiled=True)
        summed = jnp.sum(summed.reshape(NZ * NH, PIECE, classes), axis=0)
        own_labels = lax.dynamic_slice_in_dim(after(labels, partial), ((c * NZ + z) * NH + h) * PIECE, PIECE, 0)
        label_sign = 2.0 * own_labels.astype(jnp.float32) - 1.0
        fit = jax.nn.sigmoid(label_sign * summed)
        loss_weight = PENALTY * (fit - 1.0) * label_sign
        curv = PENALTY * fit * (1.0 - fit)
        both = jnp.concatenate([loss_weight, curv], axis=0)
        sent = jnp.stack([both[:, g * group:(g + 1) * group] for g in range(NY)])
        got = lax.all_to_all(sent, "y", 0, 0, tiled=True)
        slots = [lax.dynamic_index_in_dim(got, (y - k) % NY, 0, keepdims=False) for k in range(NY)]
        both = jnp.stack(slots).reshape(NY, 2, PIECE, group).transpose(1, 3, 0, 2).reshape(2, group, NY * PIECE)
        both = jnp.pad(both, ((0, 0), (0, held - group), (0, 0)))
        loss_share, curv_share = both[0], both[1]

    with jax.named_scope("rows_exchanged"):
        theirs = [turn(after(other[0], summed), "l", 1)]
        theirs.append(turn(after(other[1], theirs[0]), "l", 1))
        second = turn(after(mine[1], loss_weight), "y", 1), turn(after(mine[1], first[1]), "y", -1)
        own_weights = after(weights, loss_weight)

    def spread(share):
        count = share.shape[0]
        sent = jnp.broadcast_to(share[None], (TEAM, count, 128)).reshape(TEAM * count, 128)
        return lax.all_to_all(sent, GROUP, 0, 0, tiled=True)

    def opened(shares):
        shares = shares.reshape(TEAM, -1, 128)
        whole = shares[:, :held].transpose(1, 0, 2).reshape(held, TEAM * 128)
        return halves(whole), jnp.sum(shares[:, held:], axis=0)

    def back(near, far, k):
        return folded(times(near, blocks[k][0], 0) + times(far, blocks[k][1], 0))

    def reduce(residual, tile):
        split = [halves(v) for v in residual]
        far = turn(folded(sum(times(v, blocks[k][1], 1) for k, v in enumerate(split))), "c", 1)
        near = folded(sum(times(v, blocks[k][0], 1) for k, v in enumerate(split))) + far
        tile = tile + turn(tile, "c", 1)
        near = near.reshape(held, TEAM, 128).transpose(1, 0, 2)
        sent = jnp.concatenate([near, jnp.broadcast_to(tile[None], (TEAM, 8, 128))], axis=1)
        got = lax.all_to_all(sent.reshape(TEAM * (held + 8), 128), GROUP, 0, 0, tiled=True)
        total = jnp.sum(got.reshape(TEAM, held + 8, 128), axis=0)
        return total[:held], total[held:]

    with jax.named_scope("rows_along_y"):
        far_own = [turn(first[0], "y", 1), turn(second[1], "y", -1)]
        near = spread(after(loss_share, theirs[0]))
        third = both_ways(theirs[0])
        fourth = both_ways(theirs[1])
        far = turn(after(near, theirs[1]), "c", 1)
        far_their = [turn(third[0], "y", 1), turn(fourth[1], "y", -1)]
        blocks = []
        for k in range(PARTS):
            sides = [
                [(0.5 * v).astype(jnp.bfloat16) for v in side]
                for side in (
                    (mine[k], (first, second)[k][0], far_own[k], (first, second)[k][1]),
                    (theirs[k], (third, fourth)[k][0], far_their[k], (third, fourth)[k][1]),
                )
            ]
            blocks.append(assemble(*sides, l))

    own_weights = lax.dynamic_slice_in_dim(own_weights, y * group, group, 1).astype(jnp.float32).T
    own_weights = jnp.pad(own_weights, ((0, held - group), (0, 0)))
    own_weights = own_weights.reshape(held, NY, NL, slice_width)
    own_weights = lax.dynamic_index_in_dim(own_weights, l, 2, keepdims=False).reshape(held, NY * slice_width)

    with jax.named_scope("gradient"):
        near, far = opened(near)[0], opened(far)[0]
        residual = [
            -(own_weights[:, k * part_width:(k + 1) * part_width] + back(near, far, k)) for k in range(PARTS)
        ]

    step = [0.0] * PARTS
    direction = swing = norm_now = None
    for iteration in range(ITERS):
        with jax.named_scope("sum_over_features"):
            norm = sum(jnp.sum(v * v, axis=1) for v in residual)
            mapped, tile = reduce(residual, to_tile([norm]))
            norm_next = from_tile(tile, 0, held)
        if iteration == 0:
            direction, swing = residual, mapped
        else:
            beta = (norm_next / norm_now)[:, None]
            direction = [r + beta * d for r, d in zip(residual, direction)]
            swing = mapped + beta * swing
        norm_now = norm_next
        with jax.named_scope("spread_scaled"):
            scaled = curv_share * swing
            curved = jnp.sum(scaled * swing, axis=1)
            plain = sum(jnp.sum(d * d, axis=1) for d in direction)
            near = spread(jnp.concatenate([scaled, to_tile([curved, plain])], axis=0))
            far = turn(near, "c", 1)
            near, tile = opened(near)
            parts = [times(near, blocks[k][0], 0) for k in range(PARTS)]
            far, *parts = lax.optimization_barrier((far, *parts))
            far, far_tile = opened(far)
            tile = tile + far_tile
            alpha = (norm_now / (from_tile(tile, 1, held) + from_tile(tile, 0, held)))[:, None]
        with jax.named_scope("image"):
            step = [n + alpha * d for n, d in zip(step, direction)]
            image = [d + folded(p + times(far, blocks[k][1], 0)) for k, (d, p) in enumerate(zip(direction, parts))]
            residual = [r - alpha * i for r, i in zip(residual, image)]

    with jax.named_scope("outputs"):
        by_owner = [
            v[:, j * slice_width:(j + 1) * slice_width]
            for a, b in zip(step, residual) for j in range(per_part) for v in (a, b)
        ]
        stacked = jnp.stack(by_owner).reshape(NY, 2 * held, slice_width)
        ordered = lax.all_to_all(stacked, "y", 0, 0, tiled=True).reshape(NY, 2, held, slice_width)
        return place(ordered, group)


def solution(mesh):
    fine = Mesh(mesh.devices.reshape(SIZES), AXES)
    dp, feat = ("y", "l"), ("z", "h", "c")
    return jax.shard_map(
        shards,
        mesh=fine,
        in_specs=(P(dp, feat), P(dp), P(dp, None), P(feat, None)),
        out_specs=(P(feat, dp, None), P(feat, dp, None)),
        check_vma=False,
    )
```

```python
import functools

import jax
import jax.numpy as jnp
from jax import lax
from jax.experimental import pallas as pl
from jax.experimental.pallas import tpu as pltpu
from jax.sharding import Mesh, PartitionSpec as P

ITERS = 3
PENALTY = 8.0
SIZES = (4, 2, 4, 2, 2)
AXES = ("y", "l", "z", "h", "c")
NY, NL, NZ, NH, NC = SIZES
GROUP = ("l", "z", "h")
TEAM = NL * NZ * NH
PIECE = 32
PARTS = 2


def turn(value, axis, by):
    count = SIZES[AXES.index(axis)]
    return lax.ppermute(value, axis, [(i, (i + by) % count) for i in range(count)])


def halves(value):
    high = lax.reduce_precision(value, 8, 7)
    return jnp.concatenate([high.astype(jnp.bfloat16), (value - high).astype(jnp.bfloat16)], axis=0)


def times(both, matrix, dim):
    return lax.dot_general(both, matrix, (((1,), (dim,)), ((), ())), preferred_element_type=jnp.float32)


def folded(both):
    count = both.shape[0] // 2
    return both[:count] + both[count:]


def to_tile(vectors):
    tile = jnp.concatenate([jnp.pad(v, (0, 256 - v.shape[0])).reshape(2, 128) for v in vectors], axis=0)
    return jnp.pad(tile, ((0, 8 - tile.shape[0]), (0, 0)))


def from_tile(tile, place, count):
    return tile[2 * place:2 * place + 2].reshape(256)[:count]


def after(value, *others):
    return lax.optimization_barrier((value,) + others)[0]


def pick_kernel(slice_width, at_ref, ids_ref, fisher_ref, *refs):
    *wide_refs, picked_ref = refs
    rows = fisher_ref.shape[0]
    half = rows // 2
    ids = ids_ref[...]
    ids = jnp.where(at_ref[0] % NC == 1, jnp.concatenate([ids[:, half:], ids[:, :half]], axis=1), ids)
    places = lax.broadcasted_iota(jnp.int32, (rows, rows), 0)
    chosen = jnp.where(ids == places, 1.0, 0.0).T.astype(jnp.bfloat16)
    for s in range(NL * NY):
        side, j = s // NY, s % NY
        first = pl.multiple_of((2 * j + (at_ref[0] // NC + side) % NL) * slice_width, slice_width)
        part = jnp.dot(chosen, fisher_ref[:, pl.ds(first, slice_width)], preferred_element_type=jnp.float32)
        picked_ref[:, pl.ds(first, slice_width)] = part.astype(jnp.bfloat16)
        per_part = NY // PARTS
        columns = slice(j % per_part * slice_width, (j % per_part + 1) * slice_width)
        wide_refs[s // per_part][:, columns] = 2.0 * part


def pick(fisher, ids, at, slice_width):
    rows, width = fisher.shape
    vmem = pl.BlockSpec(memory_space=pltpu.VMEM)
    *wide, picked = pl.pallas_call(
        functools.partial(pick_kernel, slice_width),
        in_specs=[pl.BlockSpec(memory_space=pltpu.SMEM), vmem, vmem],
        out_specs=[vmem] * (NL * PARTS + 1),
        out_shape=[pltpu.VMEM((rows, NY // PARTS * slice_width), jnp.float32)] * (NL * PARTS)
        + [pltpu.VMEM((rows, width), jnp.bfloat16)],
        compiler_params=pltpu.CompilerParams(vmem_limit_bytes=24 * 2**20),
        cost_estimate=pl.CostEstimate(
            flops=2 * rows * rows * width, bytes_accessed=8 * rows * width, transcendentals=0
        ),
        name="pick",
    )(at, ids, fisher)
    return wide[:PARTS], wide[PARTS:], picked


def assemble_kernel(l_ref, *refs):
    block_refs, out_refs = refs[:-NC], refs[-NC:]
    team_half = NZ * NH
    for i, block_ref in enumerate(block_refs):
        side, slot = i // NY, i % NY
        first = pl.multiple_of((l_ref[0] + side) % NL * (team_half * NY * PIECE), team_half * NY * PIECE)
        for core, out_ref in enumerate(out_refs):
            for chip in range(team_half):
                piece = block_ref[pl.ds((core * team_half + chip) * PIECE, PIECE), :]
                out_ref[pl.ds(first + (chip * NY + slot) * PIECE, PIECE), :] = piece


def assemble(mine, theirs, l):
    rows, width = mine[0].shape
    vmem = pl.BlockSpec(memory_space=pltpu.VMEM)
    return pl.pallas_call(
        assemble_kernel,
        in_specs=[pl.BlockSpec(memory_space=pltpu.SMEM)] + [vmem] * (NL * NY),
        out_specs=[vmem] * NC,
        out_shape=[pltpu.VMEM((NL * NY * rows // NC, width), jnp.bfloat16)] * NC,
        compiler_params=pltpu.CompilerParams(vmem_limit_bytes=12 * 2**20),
        name="assemble",
    )(l.reshape(1), *mine, *theirs)


def place_kernel(group, parts_ref, *out_refs):
    for i, out_ref in enumerate(out_refs):
        for g in range(NY):
            out_ref[g * group:(g + 1) * group, 0, :] = parts_ref[g, i, :group]


def place(parts, group):
    shape = jax.ShapeDtypeStruct((NY * group, 1, parts.shape[3]), jnp.float32)
    outs = pl.pallas_call(functools.partial(place_kernel, group), out_shape=(shape, shape), name="place")(parts)
    return tuple(v.transpose(1, 2, 0) for v in outs)


def shards(fisher, sample_ids, labels, weights):
    y, l, z, h, c = [lax.axis_index(a) for a in AXES]
    rows, width = fisher.shape
    classes = labels.shape[1]
    group = classes // NY
    held = group + (-group) % 8
    slice_width = width // (NY * NL)
    half = rows // 2

    mine, other, picked = pick(fisher, sample_ids.reshape(1, rows), (l * NC + c).reshape(1), slice_width)

    per_part = NY // PARTS
    part_width = per_part * slice_width

    def both_ways(value):
        return turn(value, "y", 1), turn(value, "y", -1)

    with jax.named_scope("rows_own"):
        first = both_ways(mine[0])

    with jax.named_scope("margins"):
        partial = jnp.dot(picked, weights, preferred_element_type=jnp.float32)
        partial = partial[:half] + turn(partial[half:], "c", 1)
        summed = lax.all_to_all(partial, ("z", "h"), 0, 0, tiled=True)
        summed = jnp.sum(summed.reshape(NZ * NH, PIECE, classes), axis=0)
        own_labels = lax.dynamic_slice_in_dim(after(labels, partial), ((c * NZ + z) * NH + h) * PIECE, PIECE, 0)
        label_sign = 2.0 * own_labels.astype(jnp.float32) - 1.0
        fit = jax.nn.sigmoid(label_sign * summed)
        loss_weight = PENALTY * (fit - 1.0) * label_sign
        curv = PENALTY * fit * (1.0 - fit)
        both = jnp.concatenate([loss_weight, curv], axis=0)
        sent = jnp.stack([both[:, g * group:(g + 1) * group] for g in range(NY)])
        got = lax.all_to_all(sent, "y", 0, 0, tiled=True)
        slots = [lax.dynamic_index_in_dim(got, (y - k) % NY, 0, keepdims=False) for k in range(NY)]
        both = jnp.stack(slots).reshape(NY, 2, PIECE, group).transpose(1, 3, 0, 2).reshape(2, group, NY * PIECE)
        both = jnp.pad(both, ((0, 0), (0, held - group), (0, 0)))
        loss_share, curv_share = both[0], both[1]

    with jax.named_scope("rows_exchanged"):
        theirs = [turn(after(other[0], summed), "l", 1)]
        theirs.append(turn(after(other[1], theirs[0]), "l", 1))
        second = turn(after(mine[1], loss_weight), "y", 1), turn(after(mine[1], first[1]), "y", -1)
        own_weights = after(weights, loss_weight)

    def spread(share):
        count = share.shape[0]
        sent = jnp.broadcast_to(share[None], (TEAM, count, 128)).reshape(TEAM * count, 128)
        return lax.all_to_all(sent, GROUP, 0, 0, tiled=True)

    def opened(shares):
        shares = shares.reshape(TEAM, -1, 128)
        whole = shares[:, :held].transpose(1, 0, 2).reshape(held, TEAM * 128)
        return halves(whole), jnp.sum(shares[:, held:], axis=0)

    def back(near, far, k):
        return folded(times(near, blocks[k][0], 0) + times(far, blocks[k][1], 0))

    def reduce(residual, tile):
        split = [halves(v) for v in residual]
        far = turn(folded(sum(times(v, blocks[k][1], 1) for k, v in enumerate(split))), "c", 1)
        near = folded(sum(times(v, blocks[k][0], 1) for k, v in enumerate(split))) + far
        tile = tile + turn(tile, "c", 1)
        near = near.reshape(held, TEAM, 128).transpose(1, 0, 2)
        sent = jnp.concatenate([near, jnp.broadcast_to(tile[None], (TEAM, 8, 128))], axis=1)
        got = lax.all_to_all(sent.reshape(TEAM * (held + 8), 128), GROUP, 0, 0, tiled=True)
        total = jnp.sum(got.reshape(TEAM, held + 8, 128), axis=0)
        return total[:held], total[held:]

    with jax.named_scope("rows_along_y"):
        far_own = [turn(first[0], "y", 1), turn(second[1], "y", -1)]
        near = spread(after(loss_share, theirs[0]))
        third = both_ways(theirs[0])
        fourth = both_ways(theirs[1])
        far = turn(after(near, theirs[1]), "c", 1)
        far_their = [turn(third[0], "y", 1), turn(fourth[1], "y", -1)]
        blocks = []
        for k in range(PARTS):
            sides = [
                [(0.5 * v).astype(jnp.bfloat16) for v in side]
                for side in (
                    (mine[k], (first, second)[k][0], far_own[k], (first, second)[k][1]),
                    (theirs[k], (third, fourth)[k][0], far_their[k], (third, fourth)[k][1]),
                )
            ]
            blocks.append(assemble(*sides, l))

    own_weights = lax.dynamic_slice_in_dim(own_weights, y * group, group, 1).astype(jnp.float32).T
    own_weights = jnp.pad(own_weights, ((0, held - group), (0, 0)))
    own_weights = own_weights.reshape(held, NY, NL, slice_width)
    own_weights = lax.dynamic_index_in_dim(own_weights, l, 2, keepdims=False).reshape(held, NY * slice_width)

    with jax.named_scope("gradient"):
        near, far = opened(near)[0], opened(far)[0]
        residual = [
            -(own_weights[:, k * part_width:(k + 1) * part_width] + back(near, far, k)) for k in range(PARTS)
        ]

    step = [0.0] * PARTS
    direction = swing = norm_now = None
    for iteration in range(ITERS):
        with jax.named_scope("sum_over_features"):
            norm = sum(jnp.sum(v * v, axis=1) for v in residual)
            mapped, tile = reduce(residual, to_tile([norm]))
            norm_next = from_tile(tile, 0, held)
        if iteration == 0:
            direction, swing = residual, mapped
        else:
            beta = (norm_next / norm_now)[:, None]
            direction = [r + beta * d for r, d in zip(residual, direction)]
            swing = mapped + beta * swing
        norm_now = norm_next
        with jax.named_scope("spread_scaled"):
            scaled = curv_share * swing
            curved = jnp.sum(scaled * swing, axis=1)
            plain = sum(jnp.sum(d * d, axis=1) for d in direction)
            near = spread(jnp.concatenate([scaled, to_tile([curved, plain])], axis=0))
            far = turn(near, "c", 1)
            near, tile = opened(near)
            parts = [times(near, blocks[k][0], 0) for k in range(PARTS)]
            far, *parts = lax.optimization_barrier((far, *parts))
            far, far_tile = opened(far)
            tile = tile + far_tile
            alpha = (norm_now / (from_tile(tile, 1, held) + from_tile(tile, 0, held)))[:, None]
        with jax.named_scope("image"):
            step = [n + alpha * d for n, d in zip(step, direction)]
            image = [d + folded(p + times(far, blocks[k][1], 0)) for k, (d, p) in enumerate(zip(direction, parts))]
            residual = [r - alpha * i for r, i in zip(residual, image)]

    with jax.named_scope("outputs"):
        by_owner = [
            v[:, j * slice_width:(j + 1) * slice_width]
            for a, b in zip(step, residual) for j in range(per_part) for v in (a, b)
        ]
        stacked = jnp.stack(by_owner).reshape(NY, 2 * held, slice_width)
        ordered = lax.all_to_all(stacked, "y", 0, 0, tiled=True).reshape(NY, 2, held, slice_width)
        return place(ordered, group)


def solution(mesh):
    fine = Mesh(mesh.devices.reshape(SIZES), AXES)
    dp, feat = ("y", "l"), ("z", "h", "c")
    return jax.shard_map(
        shards,
        mesh=fine,
        in_specs=(P(dp, feat), P(dp), P(dp, None), P(feat, None)),
        out_specs=(P(feat, dp, None), P(feat, dp, None)),
        check_vma=False,
    )
```
